32 devices in a mesh: dp: 4 (over x, core), adapter: 8 (over z, y).
Axes of the slice: x: 2, y: 2, z: 4, core: 2. Of those that a mesh axis runs over, the one named last changes fastest.
Arguments:
- tokens: bfloat16 [4096, 8192], P(('dp', 'adapter')), may hold values from -6 to 6
- grad_out: bfloat16 [4096, 8192], P(('dp', 'adapter')), may hold values from -6 to 6
- down_panels: bfloat16 [16, 8192, 64], P('adapter'), may hold values from -0.0625 to 0.0625
- up_panels: bfloat16 [16, 64, 8192], P('adapter'), may hold values from -0.75 to 0.75
- seg_adapter: int32 [64], P(('dp', 'adapter')), may hold values from 0 to 15, as said below
Outputs:
- adapter_out: bfloat16 [4096, 8192], P(('dp', 'adapter'))
- grad_tokens: bfloat16 [4096, 8192], P(('dp', 'adapter'))
- grad_down: bfloat16 [16, 8192, 64], P('adapter', 'dp')
- grad_up: bfloat16 [16, 64, 8192], P('adapter', None, 'dp')
The draws below stay inside these ranges and needn't reach their ends.
Inputs may be any that keep to these rules, and one draw needn't show every extreme that they name: `seg_adapter`: adapter a is held by index a // 2 of the adapter axis. A segment of the device at index j of the adapter axis names a holder (j + k) modulo the axis's size, with k from 0 to 3; the 2 segments of one device name different holders, and in every data group some holder is named by 4 segments.
All inputs are finite; a program needn't handle non-finite values.
Results may differ from the reference program's by a relative error of at most 0.0049.
Values may be sent and summed in bfloat16 or wider, within the bound.
A program may use at most 128 MiB of HBM per device.

```python
import jax
import jax.numpy as jnp
from jax import lax

D = 8192
R = 64
ADAPT_DEV = 2
SEG = 64
SEGS = 2
REACH = 4
ADAPTERS = 16
SEGMENTS = 64
TOKENS = 4096


def draw_seg_adapter(key, part):
    owner_count = ADAPTERS // ADAPT_DEV
    device_count = SEGMENTS // SEGS
    subkeys = jax.random.split(key, 4)
    favored = jax.random.randint(subkeys[0], (), 0, owner_count)
    position = jnp.arange(device_count, dtype=jnp.int32) % owner_count
    needed = jnp.mod(favored - position, owner_count)

    def reach_order(subkey):
        return jax.random.permutation(subkey, REACH)

    def slot_order(subkey):
        return jax.random.permutation(subkey, SEGS)
    scores = jax.vmap(reach_order)(jax.random.split(subkeys[1], device_count))
    distances_all = jnp.arange(REACH, dtype=jnp.int32)[None, :]
    scores = scores + jnp.where(needed[:, None] == distances_all, REACH, 0)
    top_scores, picked_adapter = lax.top_k(scores, SEGS)
    orders = jax.vmap(slot_order)(jax.random.split(subkeys[2], device_count))
    picked_adapter = jnp.take_along_axis(picked_adapter, orders, axis=1)
    holders = jnp.mod(position[:, None] + picked_adapter, owner_count)
    local_pick = jax.random.randint(subkeys[3], (device_count, SEGS), 0, ADAPT_DEV)
    return (holders * ADAPT_DEV + local_pick).reshape(-1).astype(jnp.int32)


def block_levels(own_key, dims, shards, least, largest):
    factor_of = 1.0
    for axis_at, shards_of in shards:
        steps = jax.random.uniform(jax.random.fold_in(jax.random.fold_in(own_key, 6), axis_at), (shards_of,), jnp.float32, least / len(shards), largest / len(shards))
        factor_of = factor_of * jnp.repeat(jnp.exp(steps), dims[axis_at] // shards_of).reshape((-1,) + (1,) * (len(dims) - 1 - axis_at))
    return factor_of


def noise(rng, extent, scale, bound, shards=(), kind=jnp.bfloat16):
    loudness = block_levels(rng, extent, shards, -0.22, 0.18) if shards else 1.0
    drawn = jax.random.normal(rng, extent, jnp.float32) * scale * loudness
    return jnp.minimum(jnp.maximum(drawn, -bound), bound).astype(kind)


def setup_inputs(seed: int = 0) -> dict:
    arg_keys = jax.random.split(jax.random.key(seed), 6)
    tokens = noise(arg_keys[0], (TOKENS, D), 1.0, 6.0, ((0, 32),))
    grad_out = noise(arg_keys[1], (TOKENS, D), 1.0, 6.0, ((0, 32),))
    down_panels = noise(arg_keys[2], (ADAPTERS, D, R), D ** -0.5, 0.0625, ((0, 8),))
    up_panels = noise(arg_keys[3], (ADAPTERS, R, D), R ** -0.5, 0.75, ((0, 8),))
    seg_adapter = draw_seg_adapter(jax.random.fold_in(arg_keys[5], 71), 0)
    return {"tokens": tokens, "grad_out": grad_out, "down_panels": down_panels, "up_panels": up_panels, "seg_adapter": seg_adapter}


adapter_scale = 2.0


def reference(tokens, grad_out, down_panels, up_panels, seg_adapter):
    device_count = SEGMENTS // SEGS
    token_blocks = tokens.reshape(device_count, SEGS, SEG, D)
    grad_blocks = grad_out.reshape(device_count, SEGS, SEG, D)
    id_blocks = seg_adapter.reshape(device_count, SEGS).astype(jnp.int32)

    def one_step(totals, inputs):
        down_total, up_weight_total = totals
        token_rows, upstream, picked_adapter = inputs
        down_sel = down_panels[picked_adapter].astype(jnp.float32)
        up_weight_picked = up_panels[picked_adapter].astype(jnp.float32)
        rows_float = token_rows.astype(jnp.float32)
        upstream_gradient_wide = upstream.astype(jnp.float32)
        hidden_state = jnp.einsum("sjd,sdr->sjr", rows_float, down_sel).astype(jnp.bfloat16)
        hidden_state_wide = hidden_state.astype(jnp.float32)
        projected_output = (adapter_scale * jnp.einsum("imn,inl->iml", hidden_state_wide, up_weight_picked)).astype(jnp.bfloat16)
        hidden_gradient = (adapter_scale * jnp.einsum("yvh,ych->yvc", upstream_gradient_wide, up_weight_picked)).astype(jnp.bfloat16)
        grad_float = hidden_gradient.astype(jnp.float32)
        grad_rows = jnp.einsum("sjr,sdr->sjd", grad_float, down_sel).astype(jnp.bfloat16)
        down_total = down_total.at[picked_adapter].add(jnp.einsum("sjd,sjr->sdr", rows_float, grad_float))
        up_weight_total = up_weight_total.at[picked_adapter].add(adapter_scale * jnp.einsum("zbo,zbc->zoc", hidden_state_wide, upstream_gradient_wide))
        return (down_total, up_weight_total), (projected_output, grad_rows)

    start_totals = (jnp.zeros((ADAPTERS, D, R), jnp.float32), jnp.zeros((ADAPTERS, R, D), jnp.float32))
    (down_total, up_weight_total), (results, grads) = lax.scan(one_step, start_totals, (token_blocks, grad_blocks, id_blocks))
    return (results.reshape(TOKENS, D), grads.reshape(TOKENS, D),
            down_total.astype(jnp.bfloat16), up_weight_total.astype(jnp.bfloat16))
```

```python
import functools

import jax
import jax.numpy as jnp
from jax import lax
from jax.experimental import pallas as pl
from jax.experimental.pallas import tpu as pltpu
from jax.sharding import PartitionSpec as P

MESH = pl.DeviceIdType.MESH
scale = 2.0


def step_kernel(
    n, groups, segs, rank, reach,
    tokens, grads, pack, mask, out, gtok, gdown, gup,
    X, G, PP, M, HP, HR, HG, Hm, Gm, OB, TB, C, RA, RB, RC, RF, S1, S2, S3,
    loc, a2a_s, a2a_r, pan_s, pan_r, hp_s, hp_r, hg_s, hg_r, ob_s, ob_r,
    g_s, ra_r, rb_r, rc_r, rf_r,
):
    T, D = tokens.shape
    W = D // n
    B = PP.shape[2]
    seg_rows = T // segs
    nb = n // 2
    me = lax.axis_index("dp")
    j = lax.axis_index("adapter")
    blk, core = me // 2, me % 2
    y = j % 2
    mate = j + 1 - 2 * y
    up2, down2 = (j + 2) % groups, (j + groups - 2) % groups

    offsets = [(u, v) for u in range(1, nb) for v in range(2)] + [(0, 1)]
    peers = [(((blk + u) % nb) * 2 + (core + v) % 2) for u, v in offsets]
    senders = [(((blk + nb - u) % nb) * 2 + (core + v) % 2) for u, v in offsets]
    np_ = len(offsets)

    def rows(p):
        return pl.ds(pl.multiple_of(p * T, T), T)

    def cols(p):
        return pl.ds(pl.multiple_of(p * W, W), W)

    def rcopy(src, dst, s, r, **dev):
        return pltpu.make_async_remote_copy(
            src_ref=src, dst_ref=dst, send_sem=s, recv_sem=r, device_id=dev, device_id_type=MESH
        )

    barrier = pltpu.get_barrier_semaphore()
    for p in peers:
        pl.semaphore_signal(barrier, inc=1, device_id={"dp": p}, device_id_type=MESH)
    for h in (mate, up2, down2):
        pl.semaphore_signal(barrier, inc=1, device_id={"adapter": h}, device_id_type=MESH)
    pl.semaphore_wait(barrier, np_ + 3)

    for c in range(2):
        rcopy(pack.at[c], PP.at[c, 2], pan_s.at[0, c], pan_r.at[2, c], adapter=down2).start()

    @pl.when(y == 1)
    def _():
        for c in range(2):
            rcopy(pack.at[c], PP.at[c, 1], pan_s.at[1, c], pan_r.at[1, c], adapter=mate).start()

    for i, p in enumerate(peers):
        rcopy(mask, M.at[me], a2a_s.at[2, i], a2a_r.at[2, i], dp=p).start()
    for c, (src, dst) in enumerate(((tokens, X), (grads, G))):
        for i, p in enumerate(peers):
            rcopy(src.at[:, cols(p)], dst.at[rows(me)], a2a_s.at[c, i], a2a_r.at[c, i], dp=p).start()
    locals_ = [
        pltpu.make_async_copy(tokens.at[:, cols(me)], X.at[rows(me)], loc.at[0]),
        pltpu.make_async_copy(grads.at[:, cols(me)], G.at[rows(me)], loc.at[1]),
        pltpu.make_async_copy(pack.at[0], PP.at[0, 0], loc.at[2]),
        pltpu.make_async_copy(pack.at[1], PP.at[1, 0], loc.at[3]),
        pltpu.make_async_copy(mask, M.at[me], loc.at[4]),
    ]
    for cp in locals_:
        cp.start()
    for cp in locals_:
        cp.wait()

    def pan_wait(slot, c):
        rcopy(pack.at[c], PP.at[c, slot], pan_s.at[0, c], pan_r.at[slot, c], adapter=down2).wait_recv()

    for c in range(2):
        pan_wait(2, c)

        @pl.when(y == 0)
        def _():
            rcopy(PP.at[c, 2], PP.at[c, 1], pan_s.at[2, c], pan_r.at[1, c], adapter=mate).start()

        @pl.when(y == 1)
        def _():
            rcopy(PP.at[c, 2], PP.at[c, 3], pan_s.at[2, c], pan_r.at[3, c], adapter=mate).start()

    for c in range(2):
        pan_wait(1, c)

        @pl.when(y == 1)
        def _():
            rcopy(PP.at[c, 1], PP.at[c, 3], pan_s.at[3, c], pan_r.at[3, c], adapter=down2).start()

    for i in range(np_):
        s = senders[i]
        rcopy(mask, M.at[s], a2a_s.at[2, i], a2a_r.at[2, i], dp=peers[i]).wait_recv()
        for c, (src, dst) in enumerate(((tokens, X), (grads, G))):
            rcopy(src.at[:, cols(me)], dst.at[rows(s)], a2a_s.at[c, i], a2a_r.at[c, i], dp=peers[i]).wait_recv()

    lane = lax.broadcasted_iota(jnp.int32, (T, B), 1)
    low = lane < rank

    def row_mask(p):
        m = M[p]
        return jnp.concatenate(
            [jnp.broadcast_to(m[s:s + 1], (seg_rows, reach * B)) for s in range(segs)], axis=0
        )

    def fold(full, m):
        full = full * m
        acc = full[:, 0:B]
        for k in range(1, reach):
            acc = acc + full[:, k * B:(k + 1) * B]
        return acc + pltpu.roll(acc, rank, 1)

    nt = (((1,), (1,)), ((), ()))

    def part_dot(src, c, p):
        return lax.dot_general(
            src[rows(p), :], PP[c].reshape(reach * B, W), nt, preferred_element_type=jnp.float32
        )

    pan_wait(3, 0)

    @pl.loop(0, n)
    def _(p):
        HP[p] = fold(part_dot(X, 0, p), row_mask(p))

    pan_wait(3, 1)

    @pl.loop(0, n)
    def _(p):
        HP[p] = jnp.where(low, HP[p], scale * fold(part_dot(G, 1, p), row_mask(p)))

    for i, p in enumerate(peers):
        rcopy(HP.at[p], HR.at[me], hp_s.at[i], hp_r.at[i], dp=p).start()
    total = HP[me]
    for i in range(np_):
        s = senders[i]
        rcopy(HP.at[me], HR.at[s], hp_s.at[i], hp_r.at[i], dp=peers[i]).wait_recv()
        total = total + HR[s]
    HG[me] = total.astype(jnp.bfloat16)
    for i, p in enumerate(peers):
        rcopy(HG.at[me], HG.at[me], hg_s.at[i], hg_r.at[i], dp=p).start()
    for i in range(np_):
        s = senders[i]
        rcopy(HG.at[s], HG.at[s], hg_s.at[i], hg_r.at[i], dp=peers[i]).wait_recv()

    @pl.loop(0, n)
    def _(p):
        hg = HG[p].astype(jnp.float32)
        other = pltpu.roll(hg, rank, 1)
        h = jnp.where(low, hg, other)
        g = jnp.where(low, other, hg)
        m = row_mask(p)
        Hm[rows(p), :] = (jnp.concatenate([h] * reach, axis=1) * m).astype(jnp.bfloat16)
        Gm[rows(p), :] = (jnp.concatenate([g] * reach, axis=1) * m).astype(jnp.bfloat16)

    tile = min(W, 512)
    tn = (((0,), (0,)), ((), ()))

    def contribution(k):
        ks = slice(k * B, (k + 1) * B)

        @pl.loop(0, W // tile)
        def _(t):
            at = pl.ds(pl.multiple_of(t * tile, tile), tile)
            C[k, 0, :, at] = lax.dot_general(Gm[:, ks], X[:, at], tn, preferred_element_type=jnp.float32)
            C[k, 1, :, at] = scale * lax.dot_general(
                Hm[:, ks], G[:, at], tn, preferred_element_type=jnp.float32
            )

    def outputs(p):
        @pl.loop(0, W // tile)
        def _(t):
            at = pl.ds(pl.multiple_of(t * tile, tile), tile)
            OB[rows(p), at] = (
                scale
                * jnp.dot(
                    Hm[rows(p), :], PP[1, :, :, at].reshape(reach * B, tile),
                    preferred_element_type=jnp.float32,
                )
            ).astype(jnp.bfloat16)
            TB[rows(p), at] = jnp.dot(
                Gm[rows(p), :], PP[0, :, :, at].reshape(reach * B, tile),
                preferred_element_type=jnp.float32,
            ).astype(jnp.bfloat16)

    def send_outputs(i):
        p = peers[i]
        rcopy(OB.at[rows(p)], out.at[:, cols(me)], ob_s.at[0, i], ob_r.at[0, i], dp=p).start()
        rcopy(TB.at[rows(p)], gtok.at[:, cols(me)], ob_s.at[1, i], ob_r.at[1, i], dp=p).start()

    contribution(3)
    for c in range(2):
        S3[c] = C[3, c].astype(jnp.bfloat16)

        @pl.when(y == 0)
        def _():
            rcopy(S3.at[c], RB.at[c], g_s.at[2, c], rb_r.at[c], adapter=mate).start()

        @pl.when(y == 1)
        def _():
            rcopy(S3.at[c], RA.at[c], g_s.at[2, c], ra_r.at[c], adapter=up2).start()

    outputs(peers[0])
    send_outputs(0)
    contribution(1)

    @pl.when(y == 0)
    def _():
        for c in range(2):
            S1[c] = C[1, c].astype(jnp.bfloat16)
            rcopy(S1.at[c], RC.at[c], g_s.at[0, c], rc_r.at[c], adapter=mate).start()

    for i in range(1, np_ - 1):
        outputs(peers[i])
        send_outputs(i)
    contribution(2)

    def wait_in(ref, sem, c):
        rcopy(S3.at[c], ref.at[c], g_s.at[2, c], sem.at[c], adapter=mate).wait_recv()

    @pl.when(y == 1)
    def _():
        for c in range(2):
            wait_in(RA, ra_r, c)
            S1[c] = (C[1, c] + RA[c].astype(jnp.float32)).astype(jnp.bfloat16)
            rcopy(S1.at[c], RA.at[c], g_s.at[0, c], ra_r.at[c], adapter=mate).start()

        for c in range(2):
            wait_in(RB, rb_r, c)
            S2[c] = (C[2, c] + RB[c].astype(jnp.float32)).astype(jnp.bfloat16)
            rcopy(S2.at[c], RF.at[c], g_s.at[1, c], rf_r.at[c], adapter=up2).start()

    outputs(peers[np_ - 1])
    send_outputs(np_ - 1)
    outputs(me)
    own = [
        pltpu.make_async_copy(OB.at[rows(me)], out.at[:, cols(me)], loc.at[0]),
        pltpu.make_async_copy(TB.at[rows(me)], gtok.at[:, cols(me)], loc.at[1]),
    ]
    for cp in own:
        cp.start()
    contribution(0)

    @pl.when(y == 0)
    def _():
        for c in range(2):
            wait_in(RA, ra_r, c)
            S2[c] = (C[2, c] + RA[c].astype(jnp.float32)).astype(jnp.bfloat16)
            rcopy(S2.at[c], RF.at[c], g_s.at[1, c], rf_r.at[c], adapter=up2).start()

    @pl.when(y == 1)
    def _():
        for c in range(2):
            wait_in(RC, rc_r, c)
            C[0, c] = C[0, c] + RC[c].astype(jnp.float32)

    for c, ref in enumerate((gdown, gup)):
        wait_in(RF, rf_r, c)
        ref[...] = (C[0, c] + RF[c].astype(jnp.float32)).astype(jnp.bfloat16)

    for cp in own:
        cp.wait()
    for i, p in enumerate(peers):
        s = senders[i]
        for c, (buf, dst) in enumerate(((OB, out), (TB, gtok))):
            cp = rcopy(buf.at[rows(p)], dst.at[:, cols(s)], ob_s.at[c, i], ob_r.at[c, i], dp=p)
            cp.wait_recv()
            cp.wait_send()
        rcopy(mask, M.at[me], a2a_s.at[2, i], a2a_r.at[2, i], dp=p).wait_send()
        for c, (src, dst) in enumerate(((tokens, X), (grads, G))):
            rcopy(src.at[:, cols(p)], dst.at[rows(me)], a2a_s.at[c, i], a2a_r.at[c, i], dp=p).wait_send()
        rcopy(HP.at[p], HR.at[me], hp_s.at[i], hp_r.at[i], dp=p).wait_send()
        rcopy(HG.at[me], HG.at[me], hg_s.at[i], hg_r.at[i], dp=p).wait_send()
    for c in range(2):
        rcopy(pack.at[c], PP.at[c, 2], pan_s.at[0, c], pan_r.at[2, c], adapter=down2).wait_send()
        rcopy(PP.at[c, 2], PP.at[c, 1], pan_s.at[2, c], pan_r.at[1, c], adapter=mate).wait_send()

        @pl.when(y == 1)
        def _():
            rcopy(pack.at[c], PP.at[c, 1], pan_s.at[1, c], pan_r.at[1, c], adapter=mate).wait_send()
            rcopy(PP.at[c, 1], PP.at[c, 3], pan_s.at[3, c], pan_r.at[3, c], adapter=down2).wait_send()

        for k, buf in enumerate((S1, S2, S3)):
            rcopy(buf.at[c], RF.at[c], g_s.at[k, c], rf_r.at[c], adapter=up2).wait_send()


def on_device(n, groups, tokens, grad_out, down_panels, up_panels, seg_adapter):
    held, D, rank = down_panels.shape
    segs = seg_adapter.shape[0]
    reach = 2 * segs
    T = tokens.shape[0]
    W = D // n
    B = held * rank
    me = lax.axis_index("dp")
    position = lax.axis_index("adapter")
    down_mine = lax.dynamic_slice_in_dim(down_panels, me * W, W, 1)
    up_mine = lax.dynamic_slice_in_dim(up_panels, me * W, W, 2)
    pack = jnp.stack([jnp.transpose(down_mine, (0, 2, 1)).reshape(B, W), up_mine.reshape(B, W)])
    owner = seg_adapter // held
    pick = jnp.mod(owner - position, groups) * held + seg_adapter - owner * held
    mask = (jnp.arange(reach * B, dtype=jnp.int32)[None, :] // rank == pick[:, None]).astype(jnp.float32)
    mask = jnp.pad(mask, ((0, -segs % 8), (0, 0)))

    any_ = pl.BlockSpec(memory_space=pl.ANY)
    vmem = pl.BlockSpec(memory_space=pltpu.VMEM)
    bf, f32 = jnp.bfloat16, jnp.float32
    dma = pltpu.SemaphoreType.DMA
    k = n - 1
    rows = n * T
    result = pl.pallas_call(
        functools.partial(step_kernel, n, groups, segs, rank, reach),
        out_shape=(
            jax.ShapeDtypeStruct((T, D), bf),
            jax.ShapeDtypeStruct((T, D), bf),
            jax.ShapeDtypeStruct((B, W), bf),
            jax.ShapeDtypeStruct((B, W), bf),
        ),
        in_specs=[any_, any_, any_, vmem],
        out_specs=(any_, any_, vmem, vmem),
        scratch_shapes=[
            pltpu.VMEM((rows, W), bf),
            pltpu.VMEM((rows, W), bf),
            pltpu.VMEM((2, reach, B, W), bf),
            pltpu.VMEM((n,) + mask.shape, f32),
            pltpu.VMEM((n, T, B), f32),
            pltpu.VMEM((n, T, B), f32),
            pltpu.VMEM((n, T, B), bf),
            pltpu.VMEM((rows, reach * B), bf),
            pltpu.VMEM((rows, reach * B), bf),
            pltpu.VMEM((rows, W), bf),
            pltpu.VMEM((rows, W), bf),
            pltpu.VMEM((reach, 2, B, W), f32),
        ]
        + [pltpu.VMEM((2, B, W), bf)] * 7
        + [
            dma((5,)), dma((3, k)), dma((3, k)), dma((4, 2)), dma((4, 2)),
            dma((k,)), dma((k,)), dma((k,)), dma((k,)), dma((2, k)), dma((2, k)),
            dma((3, 2)), dma((2,)), dma((2,)), dma((2,)), dma((2,)),
        ],
        compiler_params=pltpu.CompilerParams(
            collective_id=0, has_side_effects=True, vmem_limit_bytes=50 * 1024 * 1024
        ),
        cost_estimate=pl.CostEstimate(
            flops=12 * rows * W * reach * B, bytes_accessed=16 * 2 ** 20, transcendentals=0
        ),
    )(tokens, grad_out, pack, mask)
    out, gtok, gdown, gup = result
    gdown = jnp.transpose(gdown.reshape(held, rank, W), (0, 2, 1))
    return out, gtok, gdown, gup.reshape(held, rank, W)


def solution(mesh):
    placed = (
        P(("dp", "adapter"), None),
        P(("dp", "adapter"), None),
        P("adapter", None, None),
        P("adapter", None, None),
        P(("dp", "adapter")),
    )
    return jax.shard_map(
        functools.partial(on_device, mesh.shape["dp"], mesh.shape["adapter"]),
        mesh=mesh,
        in_specs=placed,
        out_specs=(
            P(("dp", "adapter"), None),
            P(("dp", "adapter"), None),
            P("adapter", "dp", None),
            P("adapter", None, "dp"),
        ),
        check_vma=False,
    )
```

```python
import functools

import jax
import jax.numpy as jnp
from jax import lax
from jax.experimental import pallas as pl
from jax.experimental.pallas import tpu as pltpu
from jax.sharding import PartitionSpec as P

MESH = pl.DeviceIdType.MESH
scale = 2.0


def step_kernel(
    n, groups, segs, rank, reach,
    tokens, grads, down, up, mask, out, gtok, gdown, gup,
    X, G, PP, M, HP, HR, HG, Hm, Gm, OB, TB, C, RA, RB, RC, RF, S1, S2, S3,
    loc, a2a_s, a2a_r, pan_s, pan_r, hp_s, hp_r, hg_s, hg_r, ob_s, ob_r,
    g_s, ra_r, rb_r, rc_r, rf_r,
):
    T, D = tokens.shape
    W = D // n
    B = PP.shape[2]
    seg_rows = T // segs
    nb = n // 2
    me = lax.axis_index("dp")
    j = lax.axis_index("adapter")
    blk, core = me // 2, me % 2
    y = j % 2
    mate = j + 1 - 2 * y
    up2, down2 = (j + 2) % groups, (j + groups - 2) % groups

    offsets = [(u, v) for u in range(1, nb) for v in range(2)] + [(0, 1)]
    peers = [(((blk + u) % nb) * 2 + (core + v) % 2) for u, v in offsets]
    senders = [(((blk + nb - u) % nb) * 2 + (core + v) % 2) for u, v in offsets]
    np_ = len(offsets)

    def rows(p):
        return pl.ds(pl.multiple_of(p * T, T), T)

    def cols(p):
        return pl.ds(pl.multiple_of(p * W, W), W)

    def rcopy(src, dst, s, r, **dev):
        return pltpu.make_async_remote_copy(
            src_ref=src, dst_ref=dst, send_sem=s, recv_sem=r, device_id=dev, device_id_type=MESH
        )

    barrier = pltpu.get_barrier_semaphore()
    for p in peers:
        pl.semaphore_signal(barrier, inc=1, device_id={"dp": p}, device_id_type=MESH)
    for h in (mate, up2, down2):
        pl.semaphore_signal(barrier, inc=1, device_id={"adapter": h}, device_id_type=MESH)
    pl.semaphore_wait(barrier, np_ + 3)

    half = B // 2
    quarters = range(4)

    def part(ref, q, slot=None):
        at = pl.ds((q % 2) * half, half)
        return ref[q // 2].at[at, cols(me)] if slot is None else ref.at[q // 2, slot, at]

    panels = (down, up)

    def own_down(q):
        return rcopy(part(panels, q), part(PP, q, 2), pan_s.at[0, q], pan_r.at[2, q], adapter=down2)

    def own_mate(q):
        return rcopy(part(panels, q), part(PP, q, 1), pan_s.at[1, q], pan_r.at[1, q], adapter=mate)

    def relay_mate(q, slot):
        return rcopy(part(PP, q, 2), part(PP, q, slot), pan_s.at[2, q], pan_r.at[slot, q], adapter=mate)

    def relay_down(q):
        return rcopy(part(PP, q, 1), part(PP, q, 3), pan_s.at[3, q], pan_r.at[3, q], adapter=down2)

    def pan_wait(slot, q):
        rcopy(part(PP, q, 0), part(PP, q, slot), pan_s.at[0, q], pan_r.at[slot, q], adapter=down2).wait_recv()

    for q in (0, 1):
        own_down(q).start()

    @pl.when(y == 0)
    def _():
        for q in (2, 3):
            own_down(q).start()

    @pl.when(y == 1)
    def _():
        for q in (0, 1):
            own_mate(q).start()

    for i, p in enumerate(peers):
        rcopy(mask, M.at[me], a2a_s.at[2, i], a2a_r.at[2, i], dp=p).start()
    for c, (src, dst) in enumerate(((tokens, X), (grads, G))):
        for i, p in enumerate(peers):
            rcopy(src.at[:, cols(p)], dst.at[rows(me)], a2a_s.at[c, i], a2a_r.at[c, i], dp=p).start()
    locals_ = [
        pltpu.make_async_copy(tokens.at[:, cols(me)], X.at[rows(me)], loc.at[0]),
        pltpu.make_async_copy(grads.at[:, cols(me)], G.at[rows(me)], loc.at[1]),
        pltpu.make_async_copy(down.at[:, cols(me)], PP.at[0, 0], loc.at[2]),
        pltpu.make_async_copy(up.at[:, cols(me)], PP.at[1, 0], loc.at[3]),
        pltpu.make_async_copy(mask, M.at[me], loc.at[4]),
    ]
    for cp in locals_:
        cp.start()
    for cp in locals_:
        cp.wait()

    for c in range(2):
        for q in (2 * c, 2 * c + 1):
            pan_wait(2, q)

            @pl.when(y == 0)
            def _():
                relay_mate(q, 1).start()

            @pl.when(y == 1)
            def _():
                relay_mate(q, 3).start()

        for q in (2 * c, 2 * c + 1):
            pan_wait(1, q)

            @pl.when(y == 1)
            def _():
                relay_down(q).start()
                if c == 0:
                    own_down(q + 2).start()
                    own_mate(q + 2).start()

    lane_rows = reach * B

    def row_mask(p):
        m = M[p]
        return jnp.concatenate(
            [jnp.broadcast_to(m[s:s + 1], (seg_rows, lane_rows)) for s in range(segs)], axis=0
        )

    def fold(full, m):
        full = full * m
        acc = full[:, 0:B]
        for k in range(1, reach):
            acc = acc + full[:, k * B:(k + 1) * B]
        return acc + pltpu.roll(acc, rank, 1)

    nt = (((1,), (1,)), ((), ()))

    def rows_wait(c):
        src, dst = ((tokens, X), (grads, G))[c]
        for i in range(np_):
            rcopy(
                src.at[:, cols(me)], dst.at[rows(senders[i])], a2a_s.at[c, i], a2a_r.at[c, i], dp=peers[i]
            ).wait_recv()

    def send_partials(c):
        src = (X, G)[c]

        @pl.loop(0, n)
        def _(p):
            full = lax.dot_general(
                src[rows(p), :], PP[c].reshape(reach * B, W), nt, preferred_element_type=jnp.float32
            )
            HP[c, p] = (1.0, scale)[c] * fold(full, row_mask(p))

        for i, p in enumerate(peers):
            rcopy(HP.at[c, p], HR.at[c, me], hp_s.at[c, i], hp_r.at[c, i], dp=p).start()

    def send_sums(c):
        total = HP[c, me]
        for i in range(np_):
            s = senders[i]
            rcopy(HP.at[c, me], HR.at[c, s], hp_s.at[c, i], hp_r.at[c, i], dp=peers[i]).wait_recv()
            total = total + HR[c, s]
        HG[c, me] = total.astype(jnp.bfloat16)
        for i, p in enumerate(peers):
            rcopy(HG.at[c, me], HG.at[c, me], hg_s.at[c, i], hg_r.at[c, i], dp=p).start()

    def spread(c):
        for i in range(np_):
            s = senders[i]
            rcopy(HG.at[c, s], HG.at[c, s], hg_s.at[c, i], hg_r.at[c, i], dp=peers[i]).wait_recv()
        wide = (Hm, Gm)[c]

        @pl.loop(0, n)
        def _(p):
            h = HG[c, p].astype(jnp.float32)
            wide[rows(p), :] = (jnp.concatenate([h] * reach, axis=1) * row_mask(p)).astype(jnp.bfloat16)

    tile = min(W, 512)
    tn = (((0,), (0,)), ((), ()))

    def contribution(c, k):
        ks = slice(k * B, (k + 1) * B)
        wide, src = ((Gm, X), (Hm, G))[c]

        @pl.loop(0, W // tile)
        def _(t):
            at = pl.ds(pl.multiple_of(t * tile, tile), tile)
            C[k, c, :, at] = (1.0, scale)[c] * lax.dot_general(
                wide[:, ks], src[:, at], tn, preferred_element_type=jnp.float32
            )

    def outputs(c, p):
        wide, buf = ((Gm, TB), (Hm, OB))[c]

        @pl.loop(0, W // tile)
        def _(t):
            at = pl.ds(pl.multiple_of(t * tile, tile), tile)
            buf[rows(p), at] = (
                (1.0, scale)[c]
                * jnp.dot(
                    wide[rows(p), :], PP[c, :, :, at].reshape(reach * B, tile),
                    preferred_element_type=jnp.float32,
                )
            ).astype(jnp.bfloat16)

    def output_copy(c, i, at):
        buf, dst = ((TB, gtok), (OB, out))[c]
        p = peers[i]
        return rcopy(buf.at[rows(p)], dst.at[:, cols(at)], ob_s.at[c, i], ob_r.at[c, i], dp=p)

    def send_outputs(c, i):
        outputs(c, peers[i])
        output_copy(c, i, me).start()

    def own_outputs(c):
        buf, dst = ((TB, gtok), (OB, out))[c]
        outputs(c, me)
        return pltpu.make_async_copy(buf.at[rows(me)], dst.at[:, cols(me)], loc.at[c])

    def wait_in(ref, sem, c):
        rcopy(S3.at[c], ref.at[c], g_s.at[2, c], sem.at[c], adapter=mate).wait_recv()

    def start_far(c):
        contribution(c, 3)
        S3[c] = C[3, c].astype(jnp.bfloat16)

        @pl.when(y == 0)
        def _():
            rcopy(S3.at[c], RB.at[c], g_s.at[2, c], rb_r.at[c], adapter=mate).start()

        @pl.when(y == 1)
        def _():
            rcopy(S3.at[c], RA.at[c], g_s.at[2, c], ra_r.at[c], adapter=up2).start()

    def start_near(c):
        contribution(c, 1)

        @pl.when(y == 0)
        def _():
            S1[c] = C[1, c].astype(jnp.bfloat16)
            rcopy(S1.at[c], RC.at[c], g_s.at[0, c], rc_r.at[c], adapter=mate).start()

    def relay_odd(c):
        @pl.when(y == 1)
        def _():
            wait_in(RA, ra_r, c)
            S1[c] = (C[1, c] + RA[c].astype(jnp.float32)).astype(jnp.bfloat16)
            rcopy(S1.at[c], RA.at[c], g_s.at[0, c], ra_r.at[c], adapter=mate).start()
            wait_in(RB, rb_r, c)
            S2[c] = (C[2, c] + RB[c].astype(jnp.float32)).astype(jnp.bfloat16)
            rcopy(S2.at[c], RF.at[c], g_s.at[1, c], rf_r.at[c], adapter=up2).start()

    def relay_even(c):
        @pl.when(y == 0)
        def _():
            wait_in(RA, ra_r, c)
            S2[c] = (C[2, c] + RA[c].astype(jnp.float32)).astype(jnp.bfloat16)
            rcopy(S2.at[c], RF.at[c], g_s.at[1, c], rf_r.at[c], adapter=up2).start()

    for i in range(np_):
        rcopy(mask, M.at[senders[i]], a2a_s.at[2, i], a2a_r.at[2, i], dp=peers[i]).wait_recv()
    rows_wait(0)
    for q in (0, 1):
        pan_wait(3, q)
    send_partials(0)
    send_sums(0)
    spread(0)

    rows_wait(1)
    for q in (2, 3):
        pan_wait(3, q)
    send_partials(1)
    start_far(1)
    for i in range(np_ - 1):
        send_outputs(1, i)
    send_sums(1)
    start_near(1)
    send_outputs(1, np_ - 1)
    contribution(1, 2)
    spread(1)
    start_far(0)
    for i in range(np_ - 1):
        send_outputs(0, i)
    start_near(0)
    relay_odd(1)
    send_outputs(0, np_ - 1)
    contribution(0, 2)
    own = [own_outputs(1)]
    own[0].start()
    contribution(1, 0)
    relay_even(1)
    own.append(own_outputs(0))
    own[1].start()
    contribution(0, 0)
    relay_odd(0)
    relay_even(0)

    @pl.when(y == 1)
    def _():
        for c in (1, 0):
            wait_in(RC, rc_r, c)
            C[0, c] = C[0, c] + RC[c].astype(jnp.float32)

    for c, ref in ((1, gup), (0, gdown)):
        wait_in(RF, rf_r, c)
        ref[...] = (C[0, c] + RF[c].astype(jnp.float32)).astype(jnp.bfloat16)

    for cp in own:
        cp.wait()
    for i, p in enumerate(peers):
        for c in range(2):
            cp = output_copy(c, i, senders[i])
            cp.wait_recv()
            cp.wait_send()
            rcopy(HP.at[c, p], HR.at[c, me], hp_s.at[c, i], hp_r.at[c, i], dp=p).wait_send()
            rcopy(HG.at[c, me], HG.at[c, me], hg_s.at[c, i], hg_r.at[c, i], dp=p).wait_send()
        rcopy(mask, M.at[me], a2a_s.at[2, i], a2a_r.at[2, i], dp=p).wait_send()
        for c, (src, dst) in enumerate(((tokens, X), (grads, G))):
            rcopy(src.at[:, cols(p)], dst.at[rows(me)], a2a_s.at[c, i], a2a_r.at[c, i], dp=p).wait_send()
    for q in quarters:
        own_down(q).wait_send()
        relay_mate(q, 1).wait_send()

        @pl.when(y == 1)
        def _():
            own_mate(q).wait_send()
            relay_down(q).wait_send()

    for c in range(2):
        for k, buf in enumerate((S1, S2, S3)):
            rcopy(buf.at[c], RF.at[c], g_s.at[k, c], rf_r.at[c], adapter=up2).wait_send()


def on_device(n, groups, tokens, grad_out, down_panels, up_panels, seg_adapter):
    held, D, rank = down_panels.shape
    segs = seg_adapter.shape[0]
    reach = 2 * segs
    T = tokens.shape[0]
    W = D // n
    B = held * rank
    position = lax.axis_index("adapter")
    down_rows = jnp.transpose(down_panels, (0, 2, 1)).reshape(B, D)
    up_rows = up_panels.reshape(B, D)
    owner = seg_adapter // held
    pick = jnp.mod(owner - position, groups) * held + seg_adapter - owner * held
    mask = (jnp.arange(reach * B, dtype=jnp.int32)[None, :] // rank == pick[:, None]).astype(jnp.float32)
    mask = jnp.pad(mask, ((0, -segs % 8), (0, 0)))

    any_ = pl.BlockSpec(memory_space=pl.ANY)
    vmem = pl.BlockSpec(memory_space=pltpu.VMEM)
    bf, f32 = jnp.bfloat16, jnp.float32
    dma = pltpu.SemaphoreType.DMA
    k = n - 1
    rows = n * T
    result = pl.pallas_call(
        functools.partial(step_kernel, n, groups, segs, rank, reach),
        out_shape=(
            jax.ShapeDtypeStruct((T, D), bf),
            jax.ShapeDtypeStruct((T, D), bf),
            jax.ShapeDtypeStruct((B, W), bf),
            jax.ShapeDtypeStruct((B, W), bf),
        ),
        in_specs=[any_] * 4 + [vmem],
        out_specs=(vmem,) * 4,
        scratch_shapes=[
            pltpu.VMEM((rows, W), bf),
            pltpu.VMEM((rows, W), bf),
            pltpu.VMEM((2, reach, B, W), bf),
            pltpu.VMEM((n,) + mask.shape, f32),
            pltpu.VMEM((2, n, T, B), f32),
            pltpu.VMEM((2, n, T, B), f32),
            pltpu.VMEM((2, n, T, B), bf),
            pltpu.VMEM((rows, reach * B), bf),
            pltpu.VMEM((rows, reach * B), bf),
            pltpu.VMEM((rows, W), bf),
            pltpu.VMEM((rows, W), bf),
            pltpu.VMEM((reach, 2, B, W), f32),
        ]
        + [pltpu.VMEM((2, B, W), bf)] * 7
        + [
            dma((5,)), dma((3, k)), dma((3, k)), dma((4, 4)), dma((4, 4)),
            dma((2, k)), dma((2, k)), dma((2, k)), dma((2, k)), dma((2, k)), dma((2, k)),
            dma((3, 2)), dma((2,)), dma((2,)), dma((2,)), dma((2,)),
        ],
        compiler_params=pltpu.CompilerParams(
            collective_id=0, has_side_effects=True, vmem_limit_bytes=40 * 1024 * 1024
        ),
        cost_estimate=pl.CostEstimate(
            flops=12 * rows * W * reach * B, bytes_accessed=16 * 2 ** 20, transcendentals=0
        ),
    )(tokens, grad_out, down_rows, up_rows, mask)
    out, gtok, gdown, gup = result
    gdown = jnp.transpose(gdown.reshape(held, rank, W), (0, 2, 1))
    return out, gtok, gdown, gup.reshape(held, rank, W)


def solution(mesh):
    placed = (
        P(("dp", "adapter"), None),
        P(("dp", "adapter"), None),
        P("adapter", None, None),
        P("adapter", None, None),
        P(("dp", "adapter")),
    )
    return jax.shard_map(
        functools.partial(on_device, mesh.shape["dp"], mesh.shape["adapter"]),
        mesh=mesh,
        in_specs=placed,
        out_specs=(
            P(("dp", "adapter"), None),
            P(("dp", "adapter"), None),
            P("adapter", "dp", None),
            P("adapter", None, "dp"),
        ),
        check_vma=False,
    )
```

```python
import functools

import jax
import jax.numpy as jnp
from jax import lax
from jax.experimental import pallas as pl
from jax.experimental.pallas import tpu as pltpu
from jax.sharding import PartitionSpec as P

MESH = pl.DeviceIdType.MESH
scale = 2.0


def step_kernel(
    n, groups, segs, rank, reach,
    tokens, grads, pack, mask, out, gtok, gdown, gup,
    X, G, PP, M, HP, HR, HG, Hm, Gm, OB, TB, C, RA, RB, RC, RF, S1, S2, S3,
    loc, a2a_s, a2a_r, pan_s, pan_r, hp_s, hp_r, hg_s, hg_r, ob_s, ob_r,
    g_s, ra_r, rb_r, rc_r, rf_r,
):
    T, D = tokens.shape
    W = D // n
    B = PP.shape[2]
    seg_rows = T // segs
    nb = n // 2
    me = lax.axis_index("dp")
    j = lax.axis_index("adapter")
    blk, core = me // 2, me % 2
    y = j % 2
    mate = j + 1 - 2 * y
    up2, down2 = (j + 2) % groups, (j + groups - 2) % groups

    offsets = [(u, v) for u in range(1, nb) for v in range(2)] + [(0, 1)]
    peers = [(((blk + u) % nb) * 2 + (core + v) % 2) for u, v in offsets]
    senders = [(((blk + nb - u) % nb) * 2 + (core + v) % 2) for u, v in offsets]
    np_ = len(offsets)

    def rows(p):
        return pl.ds(pl.multiple_of(p * T, T), T)

    def cols(p):
        return pl.ds(pl.multiple_of(p * W, W), W)

    def rcopy(src, dst, s, r, **dev):
        return pltpu.make_async_remote_copy(
            src_ref=src, dst_ref=dst, send_sem=s, recv_sem=r, device_id=dev, device_id_type=MESH
        )

    barrier = pltpu.get_barrier_semaphore()
    for p in peers:
        pl.semaphore_signal(barrier, inc=1, device_id={"dp": p}, device_id_type=MESH)
    for h in (mate, up2, down2):
        pl.semaphore_signal(barrier, inc=1, device_id={"adapter": h}, device_id_type=MESH)
    pl.semaphore_wait(barrier, np_ + 3)

    for c in range(2):
        rcopy(pack.at[c], PP.at[c, 2], pan_s.at[0, c], pan_r.at[2, c], adapter=down2).start()

    @pl.when(y == 1)
    def _():
        for c in range(2):
            rcopy(pack.at[c], PP.at[c, 1], pan_s.at[1, c], pan_r.at[1, c], adapter=mate).start()

    for i, p in enumerate(peers):
        rcopy(mask, M.at[me], a2a_s.at[2, i], a2a_r.at[2, i], dp=p).start()
    for c, (src, dst) in enumerate(((tokens, X), (grads, G))):
        for i, p in enumerate(peers):
            rcopy(src.at[:, cols(p)], dst.at[rows(me)], a2a_s.at[c, i], a2a_r.at[c, i], dp=p).start()
    locals_ = [
        pltpu.make_async_copy(tokens.at[:, cols(me)], X.at[rows(me)], loc.at[0]),
        pltpu.make_async_copy(grads.at[:, cols(me)], G.at[rows(me)], loc.at[1]),
        pltpu.make_async_copy(pack.at[0], PP.at[0, 0], loc.at[2]),
        pltpu.make_async_copy(pack.at[1], PP.at[1, 0], loc.at[3]),
        pltpu.make_async_copy(mask, M.at[me], loc.at[4]),
    ]
    for cp in locals_:
        cp.start()
    for cp in locals_:
        cp.wait()

    def pan_wait(slot, c):
        rcopy(pack.at[c], PP.at[c, slot], pan_s.at[0, c], pan_r.at[slot, c], adapter=down2).wait_recv()

    for c in range(2):
        pan_wait(2, c)

        @pl.when(y == 0)
        def _():
            rcopy(PP.at[c, 2], PP.at[c, 1], pan_s.at[2, c], pan_r.at[1, c], adapter=mate).start()

        @pl.when(y == 1)
        def _():
            rcopy(PP.at[c, 2], PP.at[c, 3], pan_s.at[2, c], pan_r.at[3, c], adapter=mate).start()

    for c in range(2):
        pan_wait(1, c)

        @pl.when(y == 1)
        def _():
            rcopy(PP.at[c, 1], PP.at[c, 3], pan_s.at[3, c], pan_r.at[3, c], adapter=down2).start()

    for i in range(np_):
        s = senders[i]
        rcopy(mask, M.at[s], a2a_s.at[2, i], a2a_r.at[2, i], dp=peers[i]).wait_recv()
        for c, (src, dst) in enumerate(((tokens, X), (grads, G))):
            rcopy(src.at[:, cols(me)], dst.at[rows(s)], a2a_s.at[c, i], a2a_r.at[c, i], dp=peers[i]).wait_recv()

    lane = lax.broadcasted_iota(jnp.int32, (T, B), 1)
    low = lane < rank

    def row_mask(p):
        m = M[p]
        return jnp.concatenate(
            [jnp.broadcast_to(m[s:s + 1], (seg_rows, reach * B)) for s in range(segs)], axis=0
        )

    def fold(full, m):
        full = full * m
        acc = full[:, 0:B]
        for k in range(1, reach):
            acc = acc + full[:, k * B:(k + 1) * B]
        return acc + pltpu.roll(acc, rank, 1)

    nt = (((1,), (1,)), ((), ()))

    def part_dot(src, c, p):
        return lax.dot_general(
            src[rows(p), :], PP[c].reshape(reach * B, W), nt, preferred_element_type=jnp.float32
        )

    pan_wait(3, 0)

    @pl.loop(0, n)
    def _(p):
        HP[p] = fold(part_dot(X, 0, p), row_mask(p))

    pan_wait(3, 1)

    @pl.loop(0, n)
    def _(p):
        HP[p] = jnp.where(low, HP[p], scale * fold(part_dot(G, 1, p), row_mask(p)))

    for i, p in enumerate(peers):
        rcopy(HP.at[p], HR.at[me], hp_s.at[i], hp_r.at[i], dp=p).start()
    total = HP[me]
    for i in range(np_):
        s = senders[i]
        rcopy(HP.at[me], HR.at[s], hp_s.at[i], hp_r.at[i], dp=peers[i]).wait_recv()
        total = total + HR[s]
    HG[me] = total.astype(jnp.bfloat16)
    for i, p in enumerate(peers):
        rcopy(HG.at[me], HG.at[me], hg_s.at[i], hg_r.at[i], dp=p).start()
    for i in range(np_):
        s = senders[i]
        rcopy(HG.at[s], HG.at[s], hg_s.at[i], hg_r.at[i], dp=peers[i]).wait_recv()

    @pl.loop(0, n)
    def _(p):
        hg = HG[p].astype(jnp.float32)
        other = pltpu.roll(hg, rank, 1)
        h = jnp.where(low, hg, other)
        g = jnp.where(low, other, hg)
        m = row_mask(p)
        Hm[rows(p), :] = (jnp.concatenate([h] * reach, axis=1) * m).astype(jnp.bfloat16)
        Gm[rows(p), :] = (jnp.concatenate([g] * reach, axis=1) * m).astype(jnp.bfloat16)

    tile = min(W, 512)
    tn = (((0,), (0,)), ((), ()))

    def contribution(k):
        ks = slice(k * B, (k + 1) * B)

        @pl.loop(0, W // tile)
        def _(t):
            at = pl.ds(pl.multiple_of(t * tile, tile), tile)
            C[k, 0, :, at] = lax.dot_general(Gm[:, ks], X[:, at], tn, preferred_element_type=jnp.float32)
            C[k, 1, :, at] = scale * lax.dot_general(
                Hm[:, ks], G[:, at], tn, preferred_element_type=jnp.float32
            )

    def outputs(p):
        @pl.loop(0, W // tile)
        def _(t):
            at = pl.ds(pl.multiple_of(t * tile, tile), tile)
            OB[rows(p), at] = (
                scale
                * jnp.dot(
                    Hm[rows(p), :], PP[1, :, :, at].reshape(reach * B, tile),
                    preferred_element_type=jnp.float32,
                )
            ).astype(jnp.bfloat16)
            TB[rows(p), at] = jnp.dot(
                Gm[rows(p), :], PP[0, :, :, at].reshape(reach * B, tile),
                preferred_element_type=jnp.float32,
            ).astype(jnp.bfloat16)

    def send_outputs(i):
        p = peers[i]
        rcopy(OB.at[rows(p)], out.at[:, cols(me)], ob_s.at[0, i], ob_r.at[0, i], dp=p).start()
        rcopy(TB.at[rows(p)], gtok.at[:, cols(me)], ob_s.at[1, i], ob_r.at[1, i], dp=p).start()

    contribution(3)
    for c in range(2):
        S3[c] = C[3, c].astype(jnp.bfloat16)

        @pl.when(y == 0)
        def _():
            rcopy(S3.at[c], RB.at[c], g_s.at[2, c], rb_r.at[c], adapter=mate).start()

        @pl.when(y == 1)
        def _():
            rcopy(S3.at[c], RA.at[c], g_s.at[2, c], ra_r.at[c], adapter=up2).start()

    outputs(peers[0])
    send_outputs(0)
    contribution(1)

    @pl.when(y == 0)
    def _():
        for c in range(2):
            S1[c] = C[1, c].astype(jnp.bfloat16)
            rcopy(S1.at[c], RC.at[c], g_s.at[0, c], rc_r.at[c], adapter=mate).start()

    for i in range(1, np_ - 1):
        outputs(peers[i])
        send_outputs(i)
    contribution(2)

    def wait_in(ref, sem, c):
        rcopy(S3.at[c], ref.at[c], g_s.at[2, c], sem.at[c], adapter=mate).wait_recv()

    @pl.when(y == 1)
    def _():
        for c in range(2):
            wait_in(RA, ra_r, c)
            S1[c] = (C[1, c] + RA[c].astype(jnp.float32)).astype(jnp.bfloat16)
            rcopy(S1.at[c], RA.at[c], g_s.at[0, c], ra_r.at[c], adapter=mate).start()

        for c in range(2):
            wait_in(RB, rb_r, c)
            S2[c] = (C[2, c] + RB[c].astype(jnp.float32)).astype(jnp.bfloat16)
            rcopy(S2.at[c], RF.at[c], g_s.at[1, c], rf_r.at[c], adapter=up2).start()

    outputs(peers[np_ - 1])
    send_outputs(np_ - 1)
    outputs(me)
    own = [
        pltpu.make_async_copy(OB.at[rows(me)], out.at[:, cols(me)], loc.at[0]),
        pltpu.make_async_copy(TB.at[rows(me)], gtok.at[:, cols(me)], loc.at[1]),
    ]
    for cp in own:
        cp.start()
    contribution(0)

    @pl.when(y == 0)
    def _():
        for c in range(2):
            wait_in(RA, ra_r, c)
            S2[c] = (C[2, c] + RA[c].astype(jnp.float32)).astype(jnp.bfloat16)
            rcopy(S2.at[c], RF.at[c], g_s.at[1, c], rf_r.at[c], adapter=up2).start()

    @pl.when(y == 1)
    def _():
        for c in range(2):
            wait_in(RC, rc_r, c)
            C[0, c] = C[0, c] + RC[c].astype(jnp.float32)

    for c, ref in enumerate((gdown, gup)):
        wait_in(RF, rf_r, c)
        ref[...] = (C[0, c] + RF[c].astype(jnp.float32)).astype(jnp.bfloat16)

    for cp in own:
        cp.wait()
    for i, p in enumerate(peers):
        s = senders[i]
        for c, (buf, dst) in enumerate(((OB, out), (TB, gtok))):
            cp = rcopy(buf.at[rows(p)], dst.at[:, cols(s)], ob_s.at[c, i], ob_r.at[c, i], dp=p)
            cp.wait_recv()
            cp.wait_send()
        rcopy(mask, M.at[me], a2a_s.at[2, i], a2a_r.at[2, i], dp=p).wait_send()
        for c, (src, dst) in enumerate(((tokens, X), (grads, G))):
            rcopy(src.at[:, cols(p)], dst.at[rows(me)], a2a_s.at[c, i], a2a_r.at[c, i], dp=p).wait_send()
        rcopy(HP.at[p], HR.at[me], hp_s.at[i], hp_r.at[i], dp=p).wait_send()
        rcopy(HG.at[me], HG.at[me], hg_s.at[i], hg_r.at[i], dp=p).wait_send()
    for c in range(2):
        rcopy(pack.at[c], PP.at[c, 2], pan_s.at[0, c], pan_r.at[2, c], adapter=down2).wait_send()
        rcopy(PP.at[c, 2], PP.at[c, 1], pan_s.at[2, c], pan_r.at[1, c], adapter=mate).wait_send()

        @pl.when(y == 1)
        def _():
            rcopy(pack.at[c], PP.at[c, 1], pan_s.at[1, c], pan_r.at[1, c], adapter=mate).wait_send()
            rcopy(PP.at[c, 1], PP.at[c, 3], pan_s.at[3, c], pan_r.at[3, c], adapter=down2).wait_send()

        for k, buf in enumerate((S1, S2, S3)):
            rcopy(buf.at[c], RF.at[c], g_s.at[k, c], rf_r.at[c], adapter=up2).wait_send()


def on_device(n, groups, tokens, grad_out, down_panels, up_panels, seg_adapter):
    held, D, rank = down_panels.shape
    segs = seg_adapter.shape[0]
    reach = 2 * segs
    T = tokens.shape[0]
    W = D // n
    B = held * rank
    me = lax.axis_index("dp")
    position = lax.axis_index("adapter")
    down_mine = lax.dynamic_slice_in_dim(down_panels, me * W, W, 1)
    up_mine = lax.dynamic_slice_in_dim(up_panels, me * W, W, 2)
    pack = jnp.stack([jnp.transpose(down_mine, (0, 2, 1)).reshape(B, W), up_mine.reshape(B, W)])
    owner = seg_adapter // held
    pick = jnp.mod(owner - position, groups) * held + seg_adapter - owner * held
    mask = (jnp.arange(reach * B, dtype=jnp.int32)[None, :] // rank == pick[:, None]).astype(jnp.float32)
    mask = jnp.pad(mask, ((0, -segs % 8), (0, 0)))

    any_ = pl.BlockSpec(memory_space=pl.ANY)
    vmem = pl.BlockSpec(memory_space=pltpu.VMEM)
    bf, f32 = jnp.bfloat16, jnp.float32
    dma = pltpu.SemaphoreType.DMA
    k = n - 1
    rows = n * T
    result = pl.pallas_call(
        functools.partial(step_kernel, n, groups, segs, rank, reach),
        out_shape=(
            jax.ShapeDtypeStruct((T, D), bf),
            jax.ShapeDtypeStruct((T, D), bf),
            jax.ShapeDtypeStruct((B, W), bf),
            jax.ShapeDtypeStruct((B, W), bf),
        ),
        in_specs=[any_, any_, any_, vmem],
        out_specs=(vmem,) * 4,
        scratch_shapes=[
            pltpu.VMEM((rows, W), bf),
            pltpu.VMEM((rows, W), bf),
            pltpu.VMEM((2, reach, B, W), bf),
            pltpu.VMEM((n,) + mask.shape, f32),
            pltpu.VMEM((n, T, B), f32),
            pltpu.VMEM((n, T, B), f32),
            pltpu.VMEM((n, T, B), bf),
            pltpu.VMEM((rows, reach * B), bf),
            pltpu.VMEM((rows, reach * B), bf),
            pltpu.VMEM((rows, W), bf),
            pltpu.VMEM((rows, W), bf),
            pltpu.VMEM((reach, 2, B, W), f32),
        ]
        + [pltpu.VMEM((2, B, W), bf)] * 7
        + [
            dma((5,)), dma((3, k)), dma((3, k)), dma((4, 2)), dma((4, 2)),
            dma((k,)), dma((k,)), dma((k,)), dma((k,)), dma((2, k)), dma((2, k)),
            dma((3, 2)), dma((2,)), dma((2,)), dma((2,)), dma((2,)),
        ],
        compiler_params=pltpu.CompilerParams(
            collective_id=0, has_side_effects=True, vmem_limit_bytes=46 * 1024 * 1024
        ),
        cost_estimate=pl.CostEstimate(
            flops=12 * rows * W * reach * B, bytes_accessed=16 * 2 ** 20, transcendentals=0
        ),
    )(tokens, grad_out, pack, mask)
    out, gtok, gdown, gup = result
    gdown = jnp.transpose(gdown.reshape(held, rank, W), (0, 2, 1))
    return out, gtok, gdown, gup.reshape(held, rank, W)


def solution(mesh):
    placed = (
        P(("dp", "adapter"), None),
        P(("dp", "adapter"), None),
        P("adapter", None, None),
        P("adapter", None, None),
        P(("dp", "adapter")),
    )
    return jax.shard_map(
        functools.partial(on_device, mesh.shape["dp"], mesh.shape["adapter"]),
        mesh=mesh,
        in_specs=placed,
        out_specs=(
            P(("dp", "adapter"), None),
            P(("dp", "adapter"), None),
            P("adapter", "dp", None),
            P("adapter", None, "dp"),
        ),
        check_vma=False,
    )
```

```python
import functools

import jax
import jax.numpy as jnp
from jax import lax
from jax.experimental import pallas as pl
from jax.experimental.pallas import tpu as pltpu
from jax.sharding import PartitionSpec as P

MESH = pl.DeviceIdType.MESH
scale = 2.0


def step_kernel(
    n, groups, segs, rank, reach,
    tokens, grads, down, up, mask, out, gtok, gdown, gup,
    X, G, PP, M, HP, HR, HG, Hm, Gm, OB, TB, C, RA, RB, RC, RF, S1, S2, S3,
    loc, a2a_s, a2a_r, pan_s, pan_r, hp_s, hp_r, hg_s, hg_r, ob_s, ob_r,
    g_s, ra_r, rb_r, rc_r, rf_r,
):
    T, D = tokens.shape
    W = D // n
    B = PP.shape[2]
    seg_rows = T // segs
    nb = n // 2
    me = lax.axis_index("dp")
    j = lax.axis_index("adapter")
    blk, core = me // 2, me % 2
    y = j % 2
    mate = j + 1 - 2 * y
    up2, down2 = (j + 2) % groups, (j + groups - 2) % groups

    offsets = [(u, v) for u in range(1, nb) for v in range(2)] + [(0, 1)]
    peers = [(((blk + u) % nb) * 2 + (core + v) % 2) for u, v in offsets]
    senders = [(((blk + nb - u) % nb) * 2 + (core + v) % 2) for u, v in offsets]
    np_ = len(offsets)

    def rows(p):
        return pl.ds(pl.multiple_of(p * T, T), T)

    def cols(p):
        return pl.ds(pl.multiple_of(p * W, W), W)

    def rcopy(src, dst, s, r, **dev):
        return pltpu.make_async_remote_copy(
            src_ref=src, dst_ref=dst, send_sem=s, recv_sem=r, device_id=dev, device_id_type=MESH
        )

    pack = [down.at[:, cols(me)], up.at[:, cols(me)]]
    barrier = pltpu.get_barrier_semaphore()
    for p in peers:
        pl.semaphore_signal(barrier, inc=1, device_id={"dp": p}, device_id_type=MESH)
    for h in (mate, up2, down2):
        pl.semaphore_signal(barrier, inc=1, device_id={"adapter": h}, device_id_type=MESH)
    pl.semaphore_wait(barrier, np_ + 3)

    for c in range(2):
        rcopy(pack[c], PP.at[c, 2], pan_s.at[0, c], pan_r.at[2, c], adapter=down2).start()

    @pl.when(y == 1)
    def _():
        for c in range(2):
            rcopy(pack[c], PP.at[c, 1], pan_s.at[1, c], pan_r.at[1, c], adapter=mate).start()

    for i, p in enumerate(peers):
        rcopy(mask, M.at[me], a2a_s.at[2, i], a2a_r.at[2, i], dp=p).start()
    for c, (src, dst) in enumerate(((tokens, X), (grads, G))):
        for i, p in enumerate(peers):
            rcopy(src.at[:, cols(p)], dst.at[rows(me)], a2a_s.at[c, i], a2a_r.at[c, i], dp=p).start()
    locals_ = [
        pltpu.make_async_copy(tokens.at[:, cols(me)], X.at[rows(me)], loc.at[0]),
        pltpu.make_async_copy(grads.at[:, cols(me)], G.at[rows(me)], loc.at[1]),
        pltpu.make_async_copy(pack[0], PP.at[0, 0], loc.at[2]),
        pltpu.make_async_copy(pack[1], PP.at[1, 0], loc.at[3]),
        pltpu.make_async_copy(mask, M.at[me], loc.at[4]),
    ]
    for cp in locals_:
        cp.start()
    for cp in locals_:
        cp.wait()

    def pan_wait(slot, c):
        rcopy(pack[c], PP.at[c, slot], pan_s.at[0, c], pan_r.at[slot, c], adapter=down2).wait_recv()

    for c in range(2):
        pan_wait(2, c)

        @pl.when(y == 0)
        def _():
            rcopy(PP.at[c, 2], PP.at[c, 1], pan_s.at[2, c], pan_r.at[1, c], adapter=mate).start()

        @pl.when(y == 1)
        def _():
            rcopy(PP.at[c, 2], PP.at[c, 3], pan_s.at[2, c], pan_r.at[3, c], adapter=mate).start()

    for c in range(2):
        pan_wait(1, c)

        @pl.when(y == 1)
        def _():
            rcopy(PP.at[c, 1], PP.at[c, 3], pan_s.at[3, c], pan_r.at[3, c], adapter=down2).start()

    for i in range(np_):
        s = senders[i]
        rcopy(mask, M.at[s], a2a_s.at[2, i], a2a_r.at[2, i], dp=peers[i]).wait_recv()
        for c, (src, dst) in enumerate(((tokens, X), (grads, G))):
            rcopy(src.at[:, cols(me)], dst.at[rows(s)], a2a_s.at[c, i], a2a_r.at[c, i], dp=peers[i]).wait_recv()

    lane = lax.broadcasted_iota(jnp.int32, (T, B), 1)
    low = lane < rank

    def row_mask(p):
        m = M[p]
        return jnp.concatenate(
            [jnp.broadcast_to(m[s:s + 1], (seg_rows, reach * B)) for s in range(segs)], axis=0
        )

    def fold(full, m):
        full = full * m
        acc = full[:, 0:B]
        for k in range(1, reach):
            acc = acc + full[:, k * B:(k + 1) * B]
        return acc + pltpu.roll(acc, rank, 1)

    nt = (((1,), (1,)), ((), ()))

    def part_dot(src, c, p):
        return lax.dot_general(
            src[rows(p), :], PP[c].reshape(reach * B, W), nt, preferred_element_type=jnp.float32
        )

    pan_wait(3, 0)

    @pl.loop(0, n)
    def _(p):
        HP[p] = fold(part_dot(X, 0, p), row_mask(p))

    pan_wait(3, 1)

    @pl.loop(0, n)
    def _(p):
        HP[p] = jnp.where(low, HP[p], scale * fold(part_dot(G, 1, p), row_mask(p)))

    for i, p in enumerate(peers):
        rcopy(HP.at[p], HR.at[me], hp_s.at[i], hp_r.at[i], dp=p).start()
    total = HP[me]
    for i in range(np_):
        s = senders[i]
        rcopy(HP.at[me], HR.at[s], hp_s.at[i], hp_r.at[i], dp=peers[i]).wait_recv()
        total = total + HR[s]
    HG[me] = total.astype(jnp.bfloat16)
    for i, p in enumerate(peers):
        rcopy(HG.at[me], HG.at[me], hg_s.at[i], hg_r.at[i], dp=p).start()
    for i in range(np_):
        s = senders[i]
        rcopy(HG.at[s], HG.at[s], hg_s.at[i], hg_r.at[i], dp=peers[i]).wait_recv()

    @pl.loop(0, n)
    def _(p):
        hg = HG[p].astype(jnp.float32)
        other = pltpu.roll(hg, rank, 1)
        h = jnp.where(low, hg, other)
        g = jnp.where(low, other, hg)
        m = row_mask(p)
        Hm[rows(p), :] = (jnp.concatenate([h] * reach, axis=1) * m).astype(jnp.bfloat16)
        Gm[rows(p), :] = (jnp.concatenate([g] * reach, axis=1) * m).astype(jnp.bfloat16)

    tile = min(W, 512)
    tn = (((0,), (0,)), ((), ()))

    def half_contribution(k, c):
        ks = slice(k * B, (k + 1) * B)
        wide, src = ((Gm, X), (Hm, G))[c]

        @pl.loop(0, W // tile)
        def _(t):
            at = pl.ds(pl.multiple_of(t * tile, tile), tile)
            C[k, c, :, at] = (1.0, scale)[c] * lax.dot_general(
                wide[:, ks], src[:, at], tn, preferred_element_type=jnp.float32
            )

    def contribution(k):
        half_contribution(k, 0)
        half_contribution(k, 1)

    def outputs(p):
        @pl.loop(0, W // tile)
        def _(t):
            at = pl.ds(pl.multiple_of(t * tile, tile), tile)
            OB[rows(p), at] = (
                scale
                * jnp.dot(
                    Hm[rows(p), :], PP[1, :, :, at].reshape(reach * B, tile),
                    preferred_element_type=jnp.float32,
                )
            ).astype(jnp.bfloat16)
            TB[rows(p), at] = jnp.dot(
                Gm[rows(p), :], PP[0, :, :, at].reshape(reach * B, tile),
                preferred_element_type=jnp.float32,
            ).astype(jnp.bfloat16)

    def send_outputs(i):
        p = peers[i]
        rcopy(OB.at[rows(p)], out.at[:, cols(me)], ob_s.at[0, i], ob_r.at[0, i], dp=p).start()
        rcopy(TB.at[rows(p)], gtok.at[:, cols(me)], ob_s.at[1, i], ob_r.at[1, i], dp=p).start()

    for c in range(2):
        half_contribution(3, c)
        S3[c] = C[3, c].astype(jnp.bfloat16)

        @pl.when(y == 0)
        def _():
            rcopy(S3.at[c], RB.at[c], g_s.at[2, c], rb_r.at[c], adapter=mate).start()

        @pl.when(y == 1)
        def _():
            rcopy(S3.at[c], RA.at[c], g_s.at[2, c], ra_r.at[c], adapter=up2).start()

    outputs(peers[0])
    send_outputs(0)
    contribution(1)

    @pl.when(y == 0)
    def _():
        for c in range(2):
            S1[c] = C[1, c].astype(jnp.bfloat16)
            rcopy(S1.at[c], RC.at[c], g_s.at[0, c], rc_r.at[c], adapter=mate).start()

    for i in range(1, np_ - 1):
        outputs(peers[i])
        send_outputs(i)
    contribution(2)

    def wait_in(ref, sem, c):
        rcopy(S3.at[c], ref.at[c], g_s.at[2, c], sem.at[c], adapter=mate).wait_recv()

    @pl.when(y == 1)
    def _():
        for c in range(2):
            wait_in(RA, ra_r, c)
            S1[c] = (C[1, c] + RA[c].astype(jnp.float32)).astype(jnp.bfloat16)
            rcopy(S1.at[c], RA.at[c], g_s.at[0, c], ra_r.at[c], adapter=mate).start()

        for c in range(2):
            wait_in(RB, rb_r, c)
            S2[c] = (C[2, c] + RB[c].astype(jnp.float32)).astype(jnp.bfloat16)
            rcopy(S2.at[c], RF.at[c], g_s.at[1, c], rf_r.at[c], adapter=up2).start()

    outputs(peers[np_ - 1])
    send_outputs(np_ - 1)
    outputs(me)
    own = [
        pltpu.make_async_copy(OB.at[rows(me)], out.at[:, cols(me)], loc.at[0]),
        pltpu.make_async_copy(TB.at[rows(me)], gtok.at[:, cols(me)], loc.at[1]),
    ]
    for cp in own:
        cp.start()
    contribution(0)

    @pl.when(y == 0)
    def _():
        for c in range(2):
            wait_in(RA, ra_r, c)
            S2[c] = (C[2, c] + RA[c].astype(jnp.float32)).astype(jnp.bfloat16)
            rcopy(S2.at[c], RF.at[c], g_s.at[1, c], rf_r.at[c], adapter=up2).start()

    @pl.when(y == 1)
    def _():
        for c in range(2):
            wait_in(RC, rc_r, c)
            C[0, c] = C[0, c] + RC[c].astype(jnp.float32)

    for c, ref in enumerate((gdown, gup)):
        wait_in(RF, rf_r, c)
        ref[...] = (C[0, c] + RF[c].astype(jnp.float32)).astype(jnp.bfloat16)

    for cp in own:
        cp.wait()
    for i, p in enumerate(peers):
        s = senders[i]
        for c, (buf, dst) in enumerate(((OB, out), (TB, gtok))):
            cp = rcopy(buf.at[rows(p)], dst.at[:, cols(s)], ob_s.at[c, i], ob_r.at[c, i], dp=p)
            cp.wait_recv()
            cp.wait_send()
        rcopy(mask, M.at[me], a2a_s.at[2, i], a2a_r.at[2, i], dp=p).wait_send()
        for c, (src, dst) in enumerate(((tokens, X), (grads, G))):
            rcopy(src.at[:, cols(p)], dst.at[rows(me)], a2a_s.at[c, i], a2a_r.at[c, i], dp=p).wait_send()
        rcopy(HP.at[p], HR.at[me], hp_s.at[i], hp_r.at[i], dp=p).wait_send()
        rcopy(HG.at[me], HG.at[me], hg_s.at[i], hg_r.at[i], dp=p).wait_send()
    for c in range(2):
        rcopy(pack[c], PP.at[c, 2], pan_s.at[0, c], pan_r.at[2, c], adapter=down2).wait_send()
        rcopy(PP.at[c, 2], PP.at[c, 1], pan_s.at[2, c], pan_r.at[1, c], adapter=mate).wait_send()

        @pl.when(y == 1)
        def _():
            rcopy(pack[c], PP.at[c, 1], pan_s.at[1, c], pan_r.at[1, c], adapter=mate).wait_send()
            rcopy(PP.at[c, 1], PP.at[c, 3], pan_s.at[3, c], pan_r.at[3, c], adapter=down2).wait_send()

        for k, buf in enumerate((S1, S2, S3)):
            rcopy(buf.at[c], RF.at[c], g_s.at[k, c], rf_r.at[c], adapter=up2).wait_send()


def on_device(n, groups, tokens, grad_out, down_panels, up_panels, seg_adapter):
    held, D, rank = down_panels.shape
    segs = seg_adapter.shape[0]
    reach = 2 * segs
    T = tokens.shape[0]
    W = D // n
    B = held * rank
    position = lax.axis_index("adapter")
    down_rows = jnp.transpose(down_panels, (0, 2, 1)).reshape(B, D)
    up_rows = up_panels.reshape(B, D)
    owner = seg_adapter // held
    pick = jnp.mod(owner - position, groups) * held + seg_adapter - owner * held
    mask = (jnp.arange(reach * B, dtype=jnp.int32)[None, :] // rank == pick[:, None]).astype(jnp.float32)
    mask = jnp.pad(mask, ((0, -segs % 8), (0, 0)))

    any_ = pl.BlockSpec(memory_space=pl.ANY)
    vmem = pl.BlockSpec(memory_space=pltpu.VMEM)
    bf, f32 = jnp.bfloat16, jnp.float32
    dma = pltpu.SemaphoreType.DMA
    k = n - 1
    rows = n * T
    result = pl.pallas_call(
        functools.partial(step_kernel, n, groups, segs, rank, reach),
        out_shape=(
            jax.ShapeDtypeStruct((T, D), bf),
            jax.ShapeDtypeStruct((T, D), bf),
            jax.ShapeDtypeStruct((B, W), bf),
            jax.ShapeDtypeStruct((B, W), bf),
        ),
        in_specs=[any_] * 4 + [vmem],
        out_specs=(vmem,) * 4,
        scratch_shapes=[
            pltpu.VMEM((rows, W), bf),
            pltpu.VMEM((rows, W), bf),
            pltpu.VMEM((2, reach, B, W), bf),
            pltpu.VMEM((n,) + mask.shape, f32),
            pltpu.VMEM((n, T, B), f32),
            pltpu.VMEM((n, T, B), f32),
            pltpu.VMEM((n, T, B), bf),
            pltpu.VMEM((rows, reach * B), bf),
            pltpu.VMEM((rows, reach * B), bf),
            pltpu.VMEM((rows, W), bf),
            pltpu.VMEM((rows, W), bf),
            pltpu.VMEM((reach, 2, B, W), f32),
        ]
        + [pltpu.VMEM((2, B, W), bf)] * 7
        + [
            dma((5,)), dma((3, k)), dma((3, k)), dma((4, 2)), dma((4, 2)),
            dma((k,)), dma((k,)), dma((k,)), dma((k,)), dma((2, k)), dma((2, k)),
            dma((3, 2)), dma((2,)), dma((2,)), dma((2,)), dma((2,)),
        ],
        compiler_params=pltpu.CompilerParams(
            collective_id=0, has_side_effects=True, vmem_limit_bytes=48 * 1024 * 1024
        ),
        cost_estimate=pl.CostEstimate(
            flops=12 * rows * W * reach * B, bytes_accessed=16 * 2 ** 20, transcendentals=0
        ),
    )(tokens, grad_out, down_rows, up_rows, mask)
    out, gtok, gdown, gup = result
    gdown = jnp.transpose(gdown.reshape(held, rank, W), (0, 2, 1))
    return out, gtok, gdown, gup.reshape(held, rank, W)


def solution(mesh):
    placed = (
        P(("dp", "adapter"), None),
        P(("dp", "adapter"), None),
        P("adapter", None, None),
        P("adapter", None, None),
        P(("dp", "adapter")),
    )
    return jax.shard_map(
        functools.partial(on_device, mesh.shape["dp"], mesh.shape["adapter"]),
        mesh=mesh,
        in_specs=placed,
        out_specs=(
            P(("dp", "adapter"), None),
            P(("dp", "adapter"), None),
            P("adapter", "dp", None),
            P("adapter", None, "dp"),
        ),
        check_vma=False,
    )
```
